256 devices in a mesh: section: 2 (over x_lo), dp: 16 (over z, x_hi), feat: 8 (over y, core).
Axes of the slice: x: 4 (x_hi: 2, x_lo: 2; x = x_hi * 2 + x_lo), y: 4, z: 8, core: 2. Of those that a mesh axis runs over, the one named last changes fastest.
Arguments:
- context: bfloat16 [2048, 4096], P(None, ('section', 'feat')), may hold values from -6 to 6
- w_out: bfloat16 [4096, 4608], P(('section', 'feat'), 'dp')
- residual: bfloat16 [2048, 4608], P(None, 'dp'), may hold values from -6 to 6
- norm_gain: float32 [4608], P('dp'), may hold values from 0.5 to 1.5
- w_enc: bfloat16 [4608, 65536], P('dp', ('section', 'feat')), may hold values from -0.09375 to 0.09375
- b_enc: float32 [65536], P(('section', 'feat')), may hold values from -1 to 1
- w_dec: bfloat16 [65536, 4608], P(('section', 'feat'), 'dp'), may hold values from -0.125 to 0.125
- b_dec: float32 [4608], P('dp'), may hold values from -3 to 3
- block_slots: int32 [16, 16, 2], P(None, ('section', 'feat')), may hold values from -1 to 511, as said below
Outputs:
- grad_enc: bfloat16 [4608, 65536], P('dp', ('section', 'feat'))
- grad_dec: bfloat16 [65536, 4608], P(('section', 'feat'), 'dp')
The draws below stay inside these ranges and needn't reach their ends.
Inputs may be any that keep to these rules, and one draw needn't show every extreme that they name: `block_slots`: entry [t, s, :] lists distinct blocks of shard s, that is ids s * 32 to (s + 1) * 32 - 1, live ones first and -1 after them; every tile has 16 live slots in all, and some shard with all 2 slots live.
All inputs are finite; a program needn't handle non-finite values.
Results may differ from the reference program's by a relative error of at most 0.04.
Values may be sent and summed in bfloat16 or wider, within the bound.
A program may use at most 128 MiB of HBM per device.

```python
import math
import jax
import jax.numpy as jnp
from jax import lax

D = 4608
HEADS = 32
HEAD_DIM = 128
F = 65536
BLOCK = 128
SLOTS = 2
TILE = 128
SHARDS = 16
BPS = 32
ACTIVE = 16
TILES = 16
TOKENS = 2048
N_SECTION = 2
N_FEAT = 8


def draw_w_out(key, part):
    key = jax.random.fold_in(key, 11)
    key_base, key_col = jax.random.split(key)
    base_values = jax.random.normal(key_base, (HEADS * HEAD_DIM, D), jnp.float32) / math.sqrt(HEADS * HEAD_DIM)
    position = jnp.arange(D, dtype=jnp.float32) / D
    roughness = jax.random.uniform(key_col, (D,), jnp.float32, -1.15, 1.15)
    column_scale = jnp.power(3.0, position - 0.5) * jnp.exp(roughness)
    return (base_values * column_scale[None, :]).astype(jnp.bfloat16)


def draw_block_slots(key, part):
    key = jax.random.fold_in(key, 7)
    key_shift, key_sign, key_pick = jax.random.split(key, 3)
    half_slots = SLOTS // 2
    pair_count = SHARDS // 2
    shifted = jax.random.randint(key_shift, (TILES, pair_count), -half_slots, half_slots + 1)
    forced = jnp.arange(pair_count)[None, :] == (jnp.arange(TILES) % pair_count)[:, None]
    sign_values = jax.random.randint(key_sign, (TILES, 1), 0, 2) * 2 - 1
    shifted = jnp.where(forced, sign_values * half_slots, shifted)
    counts = jnp.concatenate([half_slots + shifted, half_slots - shifted], axis=1)
    scores = jax.random.randint(key_pick, (TILES, SHARDS, BPS), 0, 2 ** 20) * BPS + jnp.arange(BPS)[None, None, :]
    ranked = jnp.argsort(scores, axis=-1)[:, :, :SLOTS]
    global_ids = ranked + (jnp.arange(SHARDS) * BPS)[None, :, None]
    in_use = jnp.arange(SLOTS)[None, None, :] < counts[:, :, None]
    return jnp.where(in_use, global_ids, -1).astype(jnp.int32)


def level_of(key, extent, cuts, smallest, largest):
    gain, own = 1.0, jax.random.fold_in(key, 6)
    for axis_at, blocks in cuts:
        draws = jnp.exp(jax.random.uniform(jax.random.fold_in(own, axis_at), (blocks,), jnp.float32, smallest / len(cuts), largest / len(cuts)))
        gain = gain * jnp.repeat(draws, extent[axis_at] // blocks).reshape([-1 if axis == axis_at else 1 for axis in range(len(extent))])
    return gain


def scatter_about(stream_key, dims, spread, reach, shards=(), kind=jnp.bfloat16):
    array = jax.random.normal(stream_key, dims, jnp.float32) * spread
    if len(shards) > 0:
        array = level_of(stream_key, dims, shards, -0.22, 0.18) * array
    return jnp.clip(array, min=-reach, max=reach).astype(kind)


def setup_inputs(seed: int = 0) -> dict:
    key_list = jax.random.split(jax.random.key(seed), 10)
    return {
        "context": scatter_about(key_list[0], (TOKENS, HEADS * HEAD_DIM), 1.0, 6.0, ((1, 16),)),
        "w_out": draw_w_out(jax.random.fold_in(key_list[9], 71), 0),
        "residual": scatter_about(key_list[2], (TOKENS, D), 1.0, 6.0, ((1, 16),)),
        "norm_gain": jnp.clip(1.0 + 0.1 * jax.random.normal(key_list[3], (D,), jnp.float32), 0.5, 1.5),
        "w_enc": scatter_about(key_list[4], (D, F), D ** -0.5, 0.09375, ((0, 16), (1, 16))),
        "b_enc": jnp.clip(jax.random.uniform(key_list[5], (F,), jnp.float32, -1.0, 1.0) * level_of(key_list[5], (F,), ((0, 16),), -0.4, 0.0), -1.0, 1.0),
        "w_dec": scatter_about(key_list[6], (F, D), (ACTIVE * BLOCK) ** -0.5, 0.125, ((0, 16), (1, 16))),
        "b_dec": scatter_about(key_list[7], (D,), 0.5, 3.0, ((0, 16),), jnp.float32),
        "block_slots": draw_block_slots(jax.random.fold_in(key_list[9], 71), 0),
    }


norm_eps = 1e-06

def silu_slope(pre_act):
    sigmoid_pre = jax.nn.sigmoid(pre_act)
    return sigmoid_pre * (1.0 + pre_act * (1.0 - sigmoid_pre))

def rounded(values):
    return lax.optimization_barrier(values.astype(jnp.bfloat16)).astype(jnp.float32)

def reference(context, w_out, residual, norm_gain, w_enc, b_enc, w_dec, b_dec, block_slots):
    shard_count = N_SECTION * N_FEAT
    group_size = HEADS * HEAD_DIM // shard_count
    context_groups = context.reshape(TOKENS, shard_count, group_size).transpose(1, 0, 2)
    weight_groups = w_out.reshape(shard_count, group_size, D)

    def add_group(running_sum, pieces):
        context_part, weight_part = pieces
        partial_term = jnp.dot(context_part, weight_part, preferred_element_type=jnp.float32)
        return (running_sum + rounded(partial_term), None)
    attention, _ = lax.scan(add_group, jnp.zeros((TOKENS, D), jnp.float32), (context_groups, weight_groups))
    inv_rms = lax.rsqrt(lax.optimization_barrier(jnp.mean(attention * attention, axis=1)) + norm_eps)
    stream = (residual.astype(jnp.float32) + attention * inv_rms[:, None] * norm_gain[None, :]).astype(jnp.bfloat16)
    slot_total = shard_count * SLOTS
    enc_table = w_enc.reshape(D, F // BLOCK, BLOCK)
    dec_table = w_dec.reshape(F // BLOCK, BLOCK, D)
    bias_table = b_enc.reshape(F // BLOCK, BLOCK)

    def tile_step(accumulated, inputs):
        grad_enc, grad_dec = accumulated
        token_rows, block_ids = inputs
        live_mask = block_ids >= 0
        safe_ids = jnp.where(live_mask, block_ids, 0).astype(jnp.int32)
        mask_row = jnp.repeat(live_mask.astype(jnp.float32), BLOCK)
        weights = jnp.take(enc_table, safe_ids, axis=1).reshape(D, slot_total * BLOCK)
        bias_row = jnp.take(bias_table, safe_ids, axis=0).reshape(-1)
        pre_act = jnp.dot(token_rows, weights, preferred_element_type=jnp.float32) + bias_row[None, :]
        code_values = (jax.nn.silu(pre_act) * mask_row[None, :]).astype(jnp.bfloat16)
        decoder = jnp.take(dec_table, safe_ids, axis=0)
        per_shard = jnp.einsum('psk,skd->spd', code_values.reshape(TILE, shard_count, SLOTS * BLOCK).astype(jnp.float32), decoder.reshape(shard_count, SLOTS * BLOCK, D).astype(jnp.float32))
        rebuilt = lax.optimization_barrier(jnp.sum(rounded(per_shard), axis=0))
        residual_error = rebuilt + b_dec[None, :] - token_rows.astype(jnp.float32)
        grad_out = (residual_error / TILE).astype(jnp.bfloat16)
        flat_decoder = decoder.reshape(slot_total * BLOCK, D)
        back_values = jnp.dot(grad_out, flat_decoder.T, preferred_element_type=jnp.float32)
        grad_pre = (back_values * silu_slope(pre_act) * mask_row[None, :]).astype(jnp.bfloat16)
        dec_terms = jnp.dot(code_values.T, grad_out, preferred_element_type=jnp.float32).reshape(slot_total, BLOCK, D)
        enc_terms = jnp.dot(token_rows.T, grad_pre, preferred_element_type=jnp.float32).reshape(D, slot_total, BLOCK)
        grad_dec = grad_dec.at[safe_ids].add(dec_terms)
        grad_enc = grad_enc.at[:, safe_ids].add(enc_terms)
        return ((grad_enc, grad_dec), None)
    start_values = (jnp.zeros((D, F // BLOCK, BLOCK), jnp.float32), jnp.zeros((F // BLOCK, BLOCK, D), jnp.float32))
    tile_inputs = (stream.reshape(TILES, TILE, D), block_slots.reshape(TILES, slot_total))
    (grad_enc, grad_dec), _ = lax.scan(tile_step, start_values, tile_inputs)
    return (grad_enc.reshape(D, F).astype(jnp.bfloat16), grad_dec.reshape(F, D).astype(jnp.bfloat16))
```

```python
import functools

import jax
import jax.numpy as jnp
from jax import lax
from jax.experimental import pallas as pl
from jax.experimental.pallas import tpu as pltpu
from jax.sharding import PartitionSpec as P

MESH = pl.DeviceIdType.MESH
BF16 = jnp.bfloat16
F32 = jnp.float32

BLOCK = 128
TILE = 128
SLOTS = 2
HALVES = 2
PART = 8
Z, Y = 8, 4
LAG = 1

norm_eps = 1e-06


def dot_nn(a, b):
    return lax.dot_general(a, b, (((1,), (0,)), ((), ())), preferred_element_type=F32)


def dot_nt(a, b):
    return lax.dot_general(a, b, (((1,), (1,)), ((), ())), preferred_element_type=F32)


class Place:
    def __init__(self):
        dp, feat = lax.axis_index("dp"), lax.axis_index("feat")
        self.xl = lax.axis_index("section")
        self.z, self.xh = dp // 2, dp % 2
        self.y, self.core = feat // 2, feat % 2

    def device(self, xl=None, z=None, xh=None, y=None, core=None):
        xl = self.xl if xl is None else xl
        z = self.z if z is None else z
        xh = self.xh if xh is None else xh
        y = self.y if y is None else y
        core = self.core if core is None else core
        return (xl, z * 2 + xh, y * 2 + core)

    def sibling(self):
        return self.device(core=1 - self.core)

    def x_partner(self):
        return self.device(xh=1 - self.xh)

    def group_chip(self, code, sign):
        xl = (self.xl + code // Y) % 2
        y = (self.y + sign * (code % Y) + Y) % Y
        return xl, y

    def group_device(self, code):
        xl, y = self.group_chip(code, 1)
        return self.device(xl=xl, y=y)

    def z_device(self, step):
        return self.device(z=(self.z + step) % Z)

    def dp_device(self, code):
        return self.device(z=(self.z + code // 2) % Z, xh=(self.xh + code % 2) % 2)


def exchange_kernel(
    blocks_ref,
    live_ref,
    ctx_ref,
    w_out_ref,
    gain_ref,
    b_enc_ref,
    b_dec_ref,
    resid_hbm,
    w_enc_hbm,
    w_dec_hbm,
    stream_out,
    gp_out,
    codes_out,
    go_out,
    w_enc,
    w_dec,
    resid,
    enc_t,
    dec_t,
    cols,
    a_part,
    a_core,
    a_sum,
    a_in,
    d_part,
    d_core,
    d_sum,
    d_in,
    c_part,
    c_x,
    c_sum,
    c_in,
    e_part,
    e_x,
    e_sum,
    e_in,
    stream,
    go,
    codes,
    gp,
    power,
    power_core,
    power_in,
    local_sem,
    block_sem,
    out_sem,
    s_sem,
    r_sem,
):
    at = Place()
    me = at
    full_width = w_out_ref.shape[0] * lax.axis_size("dp")
    half_rows = w_out_ref.shape[0] // 2

    barrier = pltpu.get_barrier_semaphore()
    friends = [at.sibling()]
    friends += [at.group_device(code) for code in range(1, 8)]
    friends += [at.dp_device(code) for code in range(1, 16)]
    for friend in friends:
        pl.semaphore_signal(barrier, inc=1, device_id=friend, device_id_type=MESH)

    def block_load(src, dst, number, block):
        lanes = pl.ds(pl.multiple_of(block * BLOCK, BLOCK), BLOCK)
        return pltpu.make_async_copy(
            src.at[:, lanes], dst.at[block], block_sem.at[number, block]
        )

    def start_blocks(src, dst, number):
        def one(block, carry):
            block_load(src, dst, number, block).start()
            return carry

        lax.fori_loop(0, dst.shape[0], one, 0)

    def wait_blocks(src, dst, number):
        def one(block, carry):
            block_load(src, dst, number, block).wait()
            return carry

        lax.fori_loop(0, dst.shape[0], one, 0)

    resid_load = pltpu.make_async_copy(resid_hbm, resid, local_sem.at[0])
    resid_load.start()
    start_blocks(w_enc_hbm, w_enc, 0)
    start_blocks(w_dec_hbm, w_dec, 1)

    count = [0]
    sent = []

    def send(src, dst, device):
        slot = count[0]
        count[0] += 1
        copy = pltpu.make_async_remote_copy(
            src_ref=src,
            dst_ref=dst,
            send_sem=s_sem.at[slot],
            recv_sem=r_sem.at[slot],
            device_id=device,
            device_id_type=MESH,
        )
        copy.start()
        sent.append(copy)
        return copy

    def columns_of(ref, tile, slot):
        return ref[blocks_ref[tile, slot]]

    def rows_of(value):
        return value.reshape(2, half_rows, TILE)


    def group_reduce(h, product, part, core_in, total, arrived):
        copies = []
        for quarter in range(2):
            tiles = pl.ds(quarter * 4, 4)

            def one(j, carry, quarter=quarter):
                tile = quarter * 4 + j
                value = rows_of(product(tile).astype(BF16))
                part[h, 0, tile] = value[0]
                part[h, 1, tile] = value[1]
                return carry

            lax.fori_loop(0, 4, one, 0)
            if h == 0 and quarter == 0 and part is a_part:
                pl.semaphore_wait(barrier, len(friends))
            copies.append(
                send(part.at[h, 1 - me.core, tiles], core_in.at[h, tiles], at.sibling())
            )
        yield
        for copy in copies:
            copy.wait_recv()
        copies = []
        for code in range(1, 8):
            xl, y = at.group_chip(code, 1)
            j = xl * Y + y
            total[h, j] = (
                part[h, me.core, j].astype(F32) + core_in[h, j].astype(F32)
            ).astype(BF16)
            copies.append(
                send(total.at[h, j], arrived.at[h, code - 1], at.group_device(code))
            )
        j = me.xl * Y + me.y
        own = part[h, me.core, j].astype(F32) + core_in[h, j].astype(F32)
        yield
        for code in range(1, 8):
            copies[code - 1].wait_recv()
            own += arrived[h, code - 1].astype(F32)
        return own

    def group_gather(h, value, table):
        mine = me.xl * Y + me.y
        table[h, mine, me.core] = value
        copies = []
        for code in range(1, 8):
            region = table.at[h, mine, me.core]
            copies.append(send(region, region, at.group_device(code)))
        region = table.at[h, mine, me.core]
        forwards = [send(region, region, at.sibling())]
        yield
        for code in range(1, 8):
            copies[code - 1].wait_recv()
            xl, y = at.group_chip(code, -1)
            region = table.at[h, xl * Y + y, me.core]
            forwards.append(send(region, region, at.sibling()))
        yield
        for copy in forwards:
            copy.wait_recv()

    def dp_reduce(h, product, part, x_in, total, arrived):
        copies = []
        for quarter in range(2):
            tiles = pl.ds(quarter * 4, 4)

            def one(j, carry, quarter=quarter):
                tile = quarter * 4 + j
                first, second = product(tile)
                part[h, 0, tile] = first.astype(BF16)
                part[h, 1, tile] = second.astype(BF16)
                return carry

            lax.fori_loop(0, 4, one, 0)
            copies.append(
                send(part.at[h, 1 - me.xh, tiles], x_in.at[h, tiles], at.x_partner())
            )
        yield
        for copy in copies:
            copy.wait_recv()
        copies = []
        for step in range(1, 8):
            j = (me.z + step) % Z
            total[h, j] = (
                part[h, me.xh, j].astype(F32) + x_in[h, j].astype(F32)
            ).astype(BF16)
            copies.append(send(total.at[h, j], arrived.at[h, step - 1], at.z_device(step)))
        own = part[h, me.xh, me.z].astype(F32) + x_in[h, me.z].astype(F32)
        yield
        for step in range(1, 8):
            copies[step - 1].wait_recv()
            own += arrived[h, step - 1].astype(F32)
        return own

    def dp_gather(h, value, table):
        table[h, me.z, me.xh] = value
        region = table.at[h, me.z, me.xh]
        copies = [send(region, region, at.z_device(step)) for step in range(1, 8)]
        forwards = [send(region, region, at.x_partner())]
        yield
        for step in range(1, 8):
            copies[step - 1].wait_recv()
            region = table.at[h, (me.z - step + Z) % Z, me.xh]
            forwards.append(send(region, region, at.x_partner()))
        yield
        for copy in forwards:
            copy.wait_recv()

    outs = []

    def write_out(h, table, out, number):
        copy = pltpu.make_async_copy(
            table.at[h], out.at[h], out_sem.at[h * 4 + number]
        )
        copy.start()
        outs.append(copy)

    def half(h):
        def attention(tile):
            rows = ctx_ref[pl.ds(pl.multiple_of((h * PART + tile) * TILE, TILE), TILE), :]
            return dot_nt(w_out_ref[...], rows)

        attn = yield from group_reduce(h, attention, a_part, a_core, a_sum, a_in)
        power[h] = jnp.sum(attn * attn, axis=0, keepdims=True)
        copy = send(power.at[h], power_core.at[h], at.sibling())
        yield
        copy.wait_recv()
        power_in[h, 0] = power[h] + power_core[h]
        copies = [
            send(power_in.at[h, 0], power_in.at[h, code], at.dp_device(code))
            for code in range(1, 16)
        ]
        yield
        for copy in copies:
            copy.wait_recv()
        row_power = power_in[h, 0]
        for code in range(1, 16):
            row_power += power_in[h, code]
        inv_rms = lax.rsqrt(row_power / full_width + norm_eps)
        rows = pl.ds(pl.multiple_of(me.core * half_rows, 16), half_rows)
        if h == 0:
            resid_load.wait()
        tile = h * PART + me.xl * Y + me.y
        lanes = pl.ds(pl.multiple_of(tile * TILE, TILE), TILE)
        value = resid[rows, lanes].astype(F32) + attn * inv_rms * cols[0, rows, :]
        mine = value.astype(BF16)
        yield from group_gather(h, mine, stream)
        write_out(h, stream, stream_out, 0)

        def encode(tile):
            pair = dot_nn(enc_t[h * PART + tile], stream[h, tile].reshape(2 * half_rows, TILE))
            return pair[:BLOCK], pair[BLOCK:]

        pre = yield from dp_reduce(h, encode, c_part, c_x, c_sum, c_in)
        own_tile = h * PART + me.z
        alive = live_ref[pl.ds(own_tile * SLOTS + me.xh, 1), :]
        bias = b_enc_ref[blocks_ref[own_tile, me.xh]]
        bias = jnp.broadcast_to(bias, (BLOCK, TILE))
        pre = pre + bias.T
        sigmoid = 1.0 / (1.0 + jnp.exp(-pre))
        code_values = (pre * sigmoid * alive).astype(BF16)
        slope = sigmoid * (1.0 + pre * (1.0 - sigmoid)) * alive
        yield from dp_gather(h, code_values, codes)
        write_out(h, codes, codes_out, 1)

        def decode(tile):
            pair = codes[h, tile]
            return dot_nn(columns_of(w_dec, h * PART + tile, 0), pair[0]) + dot_nn(
                columns_of(w_dec, h * PART + tile, 1), pair[1]
            )

        rebuilt = yield from group_reduce(h, decode, d_part, d_core, d_sum, d_in)
        grad_out = (rebuilt + cols[1, rows, :] - mine.astype(F32)) / TILE
        yield from group_gather(h, grad_out.astype(BF16), go)
        write_out(h, go, go_out, 2)

        def backward(tile):
            pair = dot_nn(dec_t[h * PART + tile], go[h, tile].reshape(2 * half_rows, TILE))
            return pair[:BLOCK], pair[BLOCK:]

        back = yield from dp_reduce(h, backward, e_part, e_x, e_sum, e_in)
        yield from dp_gather(h, (back * slope).astype(BF16), gp)
        write_out(h, gp, gp_out, 3)

    def turned_blocks(table, out):
        def one(tile, carry):
            out[tile, 0:BLOCK, :] = columns_of(table, tile, 0).T
            out[tile, BLOCK : 2 * BLOCK, :] = columns_of(table, tile, 1).T
            return carry

        lax.fori_loop(0, HALVES * PART, one, 0)

    def prepare(step):
        if step == 0:
            for number, ref in enumerate((gain_ref, b_dec_ref)):
                cols[number] = jnp.broadcast_to(ref[...], (TILE, ref.shape[1])).T
            wait_blocks(w_enc_hbm, w_enc, 0)
            turned_blocks(w_enc, enc_t)
        if step == 6:
            wait_blocks(w_dec_hbm, w_dec, 1)
            turned_blocks(w_dec, dec_t)

    runs = [half(h) for h in range(HALVES)]
    running = [True] * HALVES
    step = 0
    while any(running):
        for h in range(HALVES):
            if running[h] and step >= h * LAG:
                try:
                    next(runs[h])
                except StopIteration:
                    running[h] = False
        prepare(step)
        step += 1
    for copy in sent:
        copy.wait_send()
    for copy in outs:
        copy.wait()


SENDS = 2 * (2 * (9 + 15 + 2 - 2) + 2 * (2 + 7 + 15) + 16)


def exchange(blocks, live, ctx, w_out_t, gain, b_enc, b_dec, resid_t, w_enc, w_dec_t):
    width = w_out_t.shape[0]
    half_rows = width // 2
    blocks_here = w_enc.shape[1] // BLOCK
    tiles = HALVES * PART
    vmem = pl.BlockSpec(memory_space=pltpu.VMEM)
    hbm = pl.BlockSpec(memory_space=pl.ANY)
    wide = (HALVES, PART, 2, half_rows, TILE)
    narrow = (HALVES, PART, SLOTS, BLOCK, TILE)
    group_sets = [
        pltpu.VMEM((HALVES, 2, PART, half_rows, TILE), BF16),
        pltpu.VMEM((HALVES, PART, half_rows, TILE), BF16),
        pltpu.VMEM((HALVES, PART, half_rows, TILE), BF16),
        pltpu.VMEM((HALVES, 7, half_rows, TILE), BF16),
    ]
    dp_sets = [
        pltpu.VMEM((HALVES, SLOTS, PART, BLOCK, TILE), BF16),
        pltpu.VMEM((HALVES, PART, BLOCK, TILE), BF16),
        pltpu.VMEM((HALVES, PART, BLOCK, TILE), BF16),
        pltpu.VMEM((HALVES, 7, BLOCK, TILE), BF16),
    ]
    scratch = [
        pltpu.VMEM((blocks_here, width, BLOCK), BF16),
        pltpu.VMEM((blocks_here, width, BLOCK), BF16),
        pltpu.VMEM(resid_t.shape, BF16),
        pltpu.VMEM((tiles, SLOTS * BLOCK, width), BF16),
        pltpu.VMEM((tiles, SLOTS * BLOCK, width), BF16),
        pltpu.VMEM((2, width, TILE), F32),
        *group_sets,
        *group_sets,
        *dp_sets,
        *dp_sets,
        pltpu.VMEM(wide, BF16),
        pltpu.VMEM(wide, BF16),
        pltpu.VMEM(narrow, BF16),
        pltpu.VMEM(narrow, BF16),
        pltpu.VMEM((HALVES, 1, TILE), F32),
        pltpu.VMEM((HALVES, 1, TILE), F32),
        pltpu.VMEM((HALVES, 16, 1, TILE), F32),
        pltpu.SemaphoreType.DMA((1,)),
        pltpu.SemaphoreType.DMA((2, blocks_here)),
        pltpu.SemaphoreType.DMA((HALVES * 4,)),
        pltpu.SemaphoreType.DMA((SENDS,)),
        pltpu.SemaphoreType.DMA((SENDS,)),
    ]
    return pl.pallas_call(
        exchange_kernel,
        out_shape=(
            jax.ShapeDtypeStruct(wide, BF16),
            jax.ShapeDtypeStruct(narrow, BF16),
            jax.ShapeDtypeStruct(narrow, BF16),
            jax.ShapeDtypeStruct(wide, BF16),
        ),
        in_specs=[pl.BlockSpec(memory_space=pltpu.SMEM)] + [vmem] * 6 + [hbm] * 3,
        out_specs=(hbm,) * 4,
        scratch_shapes=scratch,
        compiler_params=pltpu.CompilerParams(
            collective_id=0, has_side_effects=True, vmem_limit_bytes=52 << 20
        ),
    )(blocks, live, ctx, w_out_t, gain, b_enc, b_dec, resid_t, w_enc, w_dec_t)


def gradient_kernel(
    blocks_ref, stream, gp, codes, go, enc_out, dec_out, enc_sum, dec_sum
):
    enc_sum[...] = jnp.zeros_like(enc_sum)
    dec_sum[...] = jnp.zeros_like(dec_sum)
    width = enc_sum.shape[0]

    def one(tile, carry):
        h, j = tile // PART, tile % PART
        rows = stream[h, j].reshape(width, TILE)
        errors = go[h, j].reshape(width, TILE)
        enc = dot_nt(rows, gp[h, j].reshape(SLOTS * BLOCK, TILE))
        dec = dot_nt(errors, codes[h, j].reshape(SLOTS * BLOCK, TILE))
        for slot in range(SLOTS):
            block = blocks_ref[tile, slot]
            lanes = pl.ds(pl.multiple_of(block * BLOCK, BLOCK), BLOCK)
            mine = slice(slot * BLOCK, (slot + 1) * BLOCK)
            enc_sum[:, lanes] += enc[:, mine]
            dec_sum[:, lanes] += dec[:, mine]
        return carry

    lax.fori_loop(0, HALVES * PART, one, 0)
    enc_out[...] = enc_sum[...].astype(BF16)
    dec_out[...] = dec_sum[...].astype(BF16)


def gradients(blocks, stream, gp, codes, go, shape):
    vmem = pl.BlockSpec(memory_space=pltpu.VMEM)
    return pl.pallas_call(
        gradient_kernel,
        out_shape=(jax.ShapeDtypeStruct(shape, BF16),) * 2,
        in_specs=[pl.BlockSpec(memory_space=pltpu.SMEM)] + [vmem] * 4,
        out_specs=(vmem,) * 2,
        scratch_shapes=[pltpu.VMEM(shape, F32)] * 2,
        compiler_params=pltpu.CompilerParams(vmem_limit_bytes=48 << 20),
    )(blocks, stream, gp, codes, go)


def body(context, w_out, residual, norm_gain, w_enc, b_enc, w_dec, b_dec, block_slots):
    ids = block_slots.reshape(-1, SLOTS)
    alive = ids >= 0
    blocks = jnp.where(alive, ids % (w_enc.shape[1] // BLOCK), 0)
    live = jnp.broadcast_to(alive.reshape(-1, 1), (alive.size, TILE)).astype(F32)
    stream, gp, codes, go = exchange(
        blocks,
        live,
        context,
        w_out.T,
        norm_gain.reshape(1, -1),
        b_enc.reshape(-1, 1, BLOCK),
        b_dec.reshape(1, -1),
        residual.T,
        w_enc,
        w_dec.T,
    )
    grad_enc, grad_dec_t = gradients(blocks, stream, gp, codes, go, w_enc.shape)
    return grad_enc, grad_dec_t.T


def solution(mesh):
    placed = (
        P(None, ("section", "feat")),
        P(("section", "feat"), "dp"),
        P(None, "dp"),
        P("dp"),
        P("dp", ("section", "feat")),
        P(("section", "feat")),
        P(("section", "feat"), "dp"),
        P("dp"),
        P(None, ("section", "feat"), None),
    )
    return jax.shard_map(
        body,
        mesh=mesh,
        in_specs=placed,
        out_specs=(P("dp", ("section", "feat")), P(("section", "feat"), "dp")),
        check_vma=False,
    )
```

```python
import functools

import jax
import jax.numpy as jnp
from jax import lax
from jax.experimental import pallas as pl
from jax.experimental.pallas import tpu as pltpu
from jax.sharding import PartitionSpec as P

MESH = pl.DeviceIdType.MESH
BF16 = jnp.bfloat16
F32 = jnp.float32

BLOCK = 128
TILE = 128
SLOTS = 2
HALVES = 2
PART = 8
Z, Y = 8, 4
GROUP_ORDER = (6, 5, 7, 2, 4, 1, 3, 0)
GROUP_NEAR = (1, 3, 4, 2, 5, 7, 6)
Z_ORDER = (4, 3, 5, 2, 6, 1, 7, 0)
Z_NEAR = (1, 7, 2, 6, 3, 5, 4)
EARLY = 4
CHUNK = 2
CHORE_TIME, STEP_TIME = 0.5, 0.7

norm_eps = 1e-06


def dot_nn(a, b):
    return lax.dot_general(a, b, (((1,), (0,)), ((), ())), preferred_element_type=F32)


def dot_nt(a, b):
    return lax.dot_general(a, b, (((1,), (1,)), ((), ())), preferred_element_type=F32)


class Place:
    def __init__(self):
        dp, feat = lax.axis_index("dp"), lax.axis_index("feat")
        self.xl = lax.axis_index("section")
        self.z, self.xh = dp // 2, dp % 2
        self.y, self.core = feat // 2, feat % 2

    def device(self, xl=None, z=None, xh=None, y=None, core=None):
        xl = self.xl if xl is None else xl
        z = self.z if z is None else z
        xh = self.xh if xh is None else xh
        y = self.y if y is None else y
        core = self.core if core is None else core
        return (xl, z * 2 + xh, y * 2 + core)

    def sibling(self):
        return self.device(core=1 - self.core)

    def x_partner(self):
        return self.device(xh=1 - self.xh)

    def group_chip(self, code, sign):
        xl = (self.xl + code // Y) % 2
        y = (self.y + sign * (code % Y) + Y) % Y
        return xl, y

    def group_device(self, code):
        xl, y = self.group_chip(code, 1)
        return self.device(xl=xl, y=y)

    def z_device(self, step):
        return self.device(z=(self.z + step) % Z)

    def dp_device(self, code):
        return self.device(z=(self.z + code // 2) % Z, xh=(self.xh + code % 2) % 2)


def exchange_kernel(
    blocks_ref,
    live_ref,
    rows_ref,
    b_enc_ref,
    ctx_hbm,
    w_out_hbm,
    resid_hbm,
    w_enc_hbm,
    w_dec_hbm,
    stream_out,
    gp_out,
    codes_out,
    go_out,
    ctx_ref,
    w_out_ref,
    w_enc,
    w_dec,
    resid,
    enc_t,
    dec_t,
    cols,
    a_part,
    a_core,
    a_sum,
    a_in,
    d_part,
    d_core,
    d_sum,
    d_in,
    c_part,
    c_x,
    c_sum,
    c_in,
    e_part,
    e_x,
    e_sum,
    e_in,
    stream,
    go,
    codes,
    gp,
    power,
    power_core,
    power_in,
    local_sem,
    block_sem,
    out_sem,
    s_sem,
    r_sem,
):
    at = Place()
    me = at
    full_width = w_out_ref.shape[0] * lax.axis_size("dp")
    half_rows = w_out_ref.shape[0] // 2

    barrier = pltpu.get_barrier_semaphore()
    friends = [at.sibling()]
    friends += [at.group_device(code) for code in range(1, 8)]
    friends += [at.dp_device(code) for code in range(1, 16)]
    for friend in friends:
        pl.semaphore_signal(barrier, inc=1, device_id=friend, device_id_type=MESH)

    def block_load(src, dst, number, block):
        lanes = pl.ds(pl.multiple_of(block * BLOCK, BLOCK), BLOCK)
        return pltpu.make_async_copy(
            src.at[:, lanes], dst.at[block], block_sem.at[number, block]
        )

    def start_blocks(src, dst, number):
        def one(block, carry):
            block_load(src, dst, number, block).start()
            return carry

        lax.fori_loop(0, dst.shape[0], one, 0)

    def wait_blocks(src, dst, number):
        def one(block, carry):
            block_load(src, dst, number, block).wait()
            return carry

        lax.fori_loop(0, dst.shape[0], one, 0)

    loads = [
        pltpu.make_async_copy(src, dst, local_sem.at[number])
        for number, (src, dst) in enumerate(
            ((ctx_hbm, ctx_ref), (w_out_hbm, w_out_ref), (resid_hbm, resid))
        )
    ]
    for load in loads:
        load.start()
    start_blocks(w_enc_hbm, w_enc, 0)
    start_blocks(w_dec_hbm, w_dec, 1)

    count = [0]
    sent = []

    def send(src, dst, device):
        slot = count[0]
        count[0] += 1
        copy = pltpu.make_async_remote_copy(
            src_ref=src,
            dst_ref=dst,
            send_sem=s_sem.at[slot],
            recv_sem=r_sem.at[slot],
            device_id=device,
            device_id_type=MESH,
        )
        copy.start()
        sent.append(copy)
        return copy

    def columns_of(ref, tile, slot):
        return ref[blocks_ref[slot, tile]]

    def rows_of(value):
        return value.reshape(2, half_rows, TILE)


    def group_part(h, spot, product, part):
        xl, y = at.group_chip(GROUP_ORDER[spot], 1)
        value = rows_of(product(xl * Y + y).astype(BF16))
        part[h, 0, spot] = value[0]
        part[h, 1, spot] = value[1]

    def group_reduce(h, product, part, core_in, total, arrived):
        copies = []
        for first in range(0, PART, 2):
            spots = pl.ds(first, 2)
            if product is not None:
                group_part(h, first, product, part)
                group_part(h, first + 1, product, part)
            copies.append(
                send(part.at[h, 1 - me.core, spots], core_in.at[h, spots], at.sibling())
            )
        yield 1.5
        copies_on = []
        for spot, code in enumerate(GROUP_ORDER):
            if spot % 2 == 0:
                copies[spot // 2].wait_recv()
            value = part[h, me.core, spot].astype(F32) + core_in[h, spot].astype(F32)
            if code == 0:
                own = value
                continue
            total[h, spot] = value.astype(BF16)
            copies_on.append(
                send(total.at[h, spot], arrived.at[h, code - 1], at.group_device(code))
            )
        yield 5.0
        for copy, code in zip(copies_on, GROUP_ORDER):
            copy.wait_recv()
            own += arrived[h, code - 1].astype(F32)
        return own

    def group_gather(h, value, table):
        mine = me.xl * Y + me.y
        table[h, mine, me.core] = value
        region = table.at[h, mine, me.core]
        copies = [send(region, region, at.group_device(code)) for code in GROUP_NEAR]
        forwards = [send(region, region, at.sibling())]
        yield 5.0
        for copy, code in zip(copies, GROUP_NEAR):
            copy.wait_recv()
            xl, y = at.group_chip(code, -1)
            region = table.at[h, xl * Y + y, me.core]
            forwards.append(send(region, region, at.sibling()))
        yield 1.5
        for copy in forwards:
            copy.wait_recv()

    def dp_reduce(h, product, part, x_in, total, arrived):
        copies = []
        for first in range(0, PART, 2):
            for spot in (first, first + 1):
                pair = product((me.z + Z_ORDER[spot]) % Z).astype(BF16)
                part[h, 0, spot] = pair[:BLOCK]
                part[h, 1, spot] = pair[BLOCK:]
            spots = pl.ds(first, 2)
            copies.append(
                send(part.at[h, 1 - me.xh, spots], x_in.at[h, spots], at.x_partner())
            )
        yield 4.0
        copies_on = []
        for spot, step in enumerate(Z_ORDER):
            if spot % 2 == 0:
                copies[spot // 2].wait_recv()
            value = part[h, me.xh, spot].astype(F32) + x_in[h, spot].astype(F32)
            if step == 0:
                own = value
                continue
            total[h, spot] = value.astype(BF16)
            copies_on.append(
                send(total.at[h, spot], arrived.at[h, step - 1], at.z_device(step))
            )
        yield 6.0
        for copy, step in zip(copies_on, Z_ORDER):
            copy.wait_recv()
            own += arrived[h, step - 1].astype(F32)
        return own

    def dp_gather(h, value, table):
        table[h, me.z, me.xh] = value
        region = table.at[h, me.z, me.xh]
        copies = [send(region, region, at.z_device(step)) for step in Z_NEAR]
        forwards = [send(region, region, at.x_partner())]
        yield 6.0
        for copy, step in zip(copies, Z_NEAR):
            copy.wait_recv()
            region = table.at[h, (me.z - step + Z) % Z, me.xh]
            forwards.append(send(region, region, at.x_partner()))
        yield 3.0
        for copy in forwards:
            copy.wait_recv()

    outs = []

    def write_out(h, table, out, number):
        copy = pltpu.make_async_copy(
            table.at[h], out.at[h], out_sem.at[h * 4 + number]
        )
        copy.start()
        outs.append(copy)

    def half(h):
        attn = yield from group_reduce(h, None, a_part, a_core, a_sum, a_in)
        power[h] = jnp.sum(attn * attn, axis=0, keepdims=True)
        copy = send(power.at[h], power_core.at[h], at.sibling())
        yield 1.5
        copy.wait_recv()
        power_in[h, 0] = power[h] + power_core[h]
        copies = [
            send(power_in.at[h, 0], power_in.at[h, code], at.dp_device(code))
            for code in range(1, 16)
        ]
        yield 4.5
        for copy in copies:
            copy.wait_recv()
        row_power = power_in[h, 0]
        for code in range(1, 16):
            row_power += power_in[h, code]
        inv_rms = lax.rsqrt(row_power / full_width + norm_eps)
        rows = pl.ds(pl.multiple_of(me.core * half_rows, 16), half_rows)
        if h == 0:
            loads[2].wait()
        tile = h * PART + me.xl * Y + me.y
        lanes = pl.ds(pl.multiple_of(tile * TILE, TILE), TILE)
        value = resid[rows, lanes].astype(F32) + attn * inv_rms * cols[0, rows, :]
        mine = value.astype(BF16)
        yield from group_gather(h, mine, stream)
        write_out(h, stream, stream_out, 0)

        ensure(0, h)

        def encode(tile):
            rows = stream[h, tile].reshape(2 * half_rows, TILE)
            return dot_nn(enc_t[h * PART + tile], rows)

        pre = yield from dp_reduce(h, encode, c_part, c_x, c_sum, c_in)
        own_tile = h * PART + me.z
        alive = live_ref[me.xh, pl.ds(own_tile, 1), :]
        bias = b_enc_ref[blocks_ref[me.xh, own_tile]]
        bias = jnp.broadcast_to(bias, (BLOCK, TILE))
        pre = pre + bias.T
        sigmoid = 1.0 / (1.0 + jnp.exp(-pre))
        code_values = (pre * sigmoid * alive).astype(BF16)
        slope = sigmoid * (1.0 + pre * (1.0 - sigmoid)) * alive
        yield from dp_gather(h, code_values, codes)
        write_out(h, codes, codes_out, 1)

        if 1 not in waited:
            waited.add(1)
            wait_blocks(w_dec_hbm, w_dec, 1)

        def decode(tile):
            pair = codes[h, tile]
            return dot_nn(columns_of(w_dec, h * PART + tile, 0), pair[0]) + dot_nn(
                columns_of(w_dec, h * PART + tile, 1), pair[1]
            )

        rebuilt = yield from group_reduce(h, decode, d_part, d_core, d_sum, d_in)
        grad_out = (rebuilt + cols[1, rows, :] - mine.astype(F32)) / TILE
        yield from group_gather(h, grad_out.astype(BF16), go)
        write_out(h, go, go_out, 2)

        ensure(1, h)

        def backward(tile):
            rows = go[h, tile].reshape(2 * half_rows, TILE)
            return dot_nn(dec_t[h * PART + tile], rows)

        back = yield from dp_reduce(h, backward, e_part, e_x, e_sum, e_in)
        yield from dp_gather(h, (back * slope).astype(BF16), gp)
        write_out(h, gp, gp_out, 3)

    def turn(table, out, first):
        def one(tile, carry):
            out[tile, 0:BLOCK, :] = columns_of(table, tile, 0).T
            out[tile, BLOCK : 2 * BLOCK, :] = columns_of(table, tile, 1).T
            return carry

        lax.fori_loop(first, first + CHUNK, one, 0)

    waited = set()
    chores = [
        (number, first)
        for number in range(2)
        for first in range(0, HALVES * PART, CHUNK)
    ]

    def chore():
        number, first = chores.pop(0)
        src, table, out = (
            (w_enc_hbm, w_enc, enc_t),
            (w_dec_hbm, w_dec, dec_t),
        )[number]
        if number not in waited:
            waited.add(number)
            wait_blocks(src, table, number)
        turn(table, out, first)

    def ensure(number, h):
        while chores and chores[0] < (number, (h + 1) * PART):
            chore()

    loads[0].wait()
    loads[1].wait()
    for h in range(HALVES):

        def attention(tile, h=h):
            rows = ctx_ref[pl.ds(pl.multiple_of((h * PART + tile) * TILE, TILE), TILE), :]
            return dot_nt(w_out_ref[...], rows)

        for spot in range(PART):
            group_part(h, spot, attention, a_part)
    for number in range(2):
        row = rows_ref[pl.ds(number, 1), :]
        cols[number] = jnp.broadcast_to(row, (TILE, row.shape[1])).T
    for _ in range(EARLY):
        chore()
    pl.semaphore_wait(barrier, len(friends))
    runs = [half(h) for h in range(HALVES)]
    due = [float(h) for h in range(HALVES)]
    clock = 0.0
    started = False
    while runs:
        h = min(range(len(runs)), key=lambda i: due[i])
        while chores and clock + CHORE_TIME < due[h] and started:
            chore()
            clock += CHORE_TIME
        clock = max(clock, due[h]) + STEP_TIME
        try:
            due[h] = clock + next(runs[h])
        except StopIteration:
            del runs[h], due[h]
        started = True
    for copy in sent:
        copy.wait_send()
    for copy in outs:
        copy.wait()


SENDS = HALVES * (4 * (4 + 7 + 15) + 16)


def exchange(blocks, live, ctx, w_out_t, gain_bias, b_enc, resid_t, w_enc, w_dec_t):
    width = w_out_t.shape[0]
    half_rows = width // 2
    blocks_here = w_enc.shape[1] // BLOCK
    tiles = HALVES * PART
    vmem = pl.BlockSpec(memory_space=pltpu.VMEM)
    hbm = pl.BlockSpec(memory_space=pl.ANY)
    wide = (HALVES, PART, 2, half_rows, TILE)
    narrow = (HALVES, PART, SLOTS, BLOCK, TILE)
    group_sets = [
        pltpu.VMEM((HALVES, 2, PART, half_rows, TILE), BF16),
        pltpu.VMEM((HALVES, PART, half_rows, TILE), BF16),
        pltpu.VMEM((HALVES, PART, half_rows, TILE), BF16),
        pltpu.VMEM((HALVES, 7, half_rows, TILE), BF16),
    ]
    dp_sets = [
        pltpu.VMEM((HALVES, SLOTS, PART, BLOCK, TILE), BF16),
        pltpu.VMEM((HALVES, PART, BLOCK, TILE), BF16),
        pltpu.VMEM((HALVES, PART, BLOCK, TILE), BF16),
        pltpu.VMEM((HALVES, 7, BLOCK, TILE), BF16),
    ]
    scratch = [
        pltpu.VMEM(ctx.shape, BF16),
        pltpu.VMEM(w_out_t.shape, BF16),
        pltpu.VMEM((blocks_here, width, BLOCK), BF16),
        pltpu.VMEM((blocks_here, width, BLOCK), BF16),
        pltpu.VMEM(resid_t.shape, BF16),
        pltpu.VMEM((tiles, SLOTS * BLOCK, width), BF16),
        pltpu.VMEM((tiles, SLOTS * BLOCK, width), BF16),
        pltpu.VMEM((2, width, TILE), F32),
        *group_sets,
        *group_sets,
        *dp_sets,
        *dp_sets,
        pltpu.VMEM(wide, BF16),
        pltpu.VMEM(wide, BF16),
        pltpu.VMEM(narrow, BF16),
        pltpu.VMEM(narrow, BF16),
        pltpu.VMEM((HALVES, 1, TILE), F32),
        pltpu.VMEM((HALVES, 1, TILE), F32),
        pltpu.VMEM((HALVES, 16, 1, TILE), F32),
        pltpu.SemaphoreType.DMA((3,)),
        pltpu.SemaphoreType.DMA((2, blocks_here)),
        pltpu.SemaphoreType.DMA((HALVES * 4,)),
        pltpu.SemaphoreType.DMA((SENDS,)),
        pltpu.SemaphoreType.DMA((SENDS,)),
    ]
    return pl.pallas_call(
        exchange_kernel,
        out_shape=(
            jax.ShapeDtypeStruct(wide, BF16),
            jax.ShapeDtypeStruct(narrow, BF16),
            jax.ShapeDtypeStruct(narrow, BF16),
            jax.ShapeDtypeStruct(wide, BF16),
        ),
        in_specs=[pl.BlockSpec(memory_space=pltpu.SMEM)] + [vmem] * 3 + [hbm] * 5,
        out_specs=(hbm,) * 4,
        scratch_shapes=scratch,
        compiler_params=pltpu.CompilerParams(
            collective_id=0, has_side_effects=True, vmem_limit_bytes=52 << 20
        ),
    )(blocks, live, gain_bias, b_enc, ctx, w_out_t, resid_t, w_enc, w_dec_t)


def gradient_kernel(
    blocks_ref,
    stream_hbm,
    gp_hbm,
    codes_hbm,
    go_hbm,
    enc_out,
    dec_out,
    stream,
    gp,
    codes,
    go,
    total,
    result,
    in_sem,
    out_sem,
):
    loads = [
        pltpu.make_async_copy(src, dst, in_sem.at[number])
        for number, (src, dst) in enumerate(
            ((codes_hbm, codes), (go_hbm, go), (stream_hbm, stream), (gp_hbm, gp))
        )
    ]
    for load in loads:
        load.start()
    total[...] = jnp.zeros_like(total)
    width, features = total.shape[1:]
    share = features // 4
    writes = []
    for number, (left, right, out) in enumerate(
        ((go, codes, dec_out), (stream, gp, enc_out))
    ):
        loads[2 * number].wait()
        loads[2 * number + 1].wait()

        def one(tile, carry, number=number, left=left, right=right):
            h, j = tile // PART, tile % PART
            terms = dot_nt(
                left[h, j].reshape(width, TILE), right[h, j].reshape(SLOTS * BLOCK, TILE)
            )
            for slot in range(SLOTS):
                block = blocks_ref[slot, tile]
                lanes = pl.ds(pl.multiple_of(block * BLOCK, BLOCK), BLOCK)
                total[number, :, lanes] += terms[:, slot * BLOCK : (slot + 1) * BLOCK]
            return carry

        lax.fori_loop(0, HALVES * PART, one, 0, unroll=4)
        for quarter in range(4):
            lanes = pl.ds(quarter * share, share)
            result[number, :, lanes] = total[number, :, lanes].astype(BF16)
            write = pltpu.make_async_copy(
                result.at[number, :, lanes], out.at[:, lanes], out_sem.at[number, quarter]
            )
            write.start()
            writes.append(write)
    for write in writes:
        write.wait()


def gradients(blocks, stream, gp, codes, go, shape):
    hbm = pl.BlockSpec(memory_space=pl.ANY)
    return pl.pallas_call(
        gradient_kernel,
        out_shape=(jax.ShapeDtypeStruct(shape, BF16),) * 2,
        in_specs=[pl.BlockSpec(memory_space=pltpu.SMEM)] + [hbm] * 4,
        out_specs=(hbm,) * 2,
        scratch_shapes=[
            pltpu.VMEM(stream.shape, BF16),
            pltpu.VMEM(gp.shape, BF16),
            pltpu.VMEM(codes.shape, BF16),
            pltpu.VMEM(go.shape, BF16),
            pltpu.VMEM((2, *shape), F32),
            pltpu.VMEM((2, *shape), BF16),
            pltpu.SemaphoreType.DMA((4,)),
            pltpu.SemaphoreType.DMA((2, 4)),
        ],
        compiler_params=pltpu.CompilerParams(vmem_limit_bytes=52 << 20),
    )(blocks, stream, gp, codes, go)


def body(context, w_out, residual, norm_gain, w_enc, b_enc, w_dec, b_dec, block_slots):
    ids = block_slots[:, 0, :].T
    alive = ids >= 0
    blocks = jnp.where(alive, ids % (w_enc.shape[1] // BLOCK), 0)
    live = jnp.broadcast_to(alive[:, :, None], (*alive.shape, TILE)).astype(F32)
    stream, gp, codes, go = exchange(
        blocks,
        live,
        context,
        w_out.T,
        jnp.stack([norm_gain, b_dec]),
        b_enc.reshape(-1, 1, BLOCK),
        residual.T,
        w_enc,
        w_dec.T,
    )
    grad_enc, grad_dec_t = gradients(blocks, stream, gp, codes, go, w_enc.shape)
    return grad_enc, grad_dec_t.T


def solution(mesh):
    placed = (
        P(None, ("section", "feat")),
        P(("section", "feat"), "dp"),
        P(None, "dp"),
        P("dp"),
        P("dp", ("section", "feat")),
        P(("section", "feat")),
        P(("section", "feat"), "dp"),
        P("dp"),
        P(None, ("section", "feat"), None),
    )
    return jax.shard_map(
        body,
        mesh=mesh,
        in_specs=placed,
        out_specs=(P("dp", ("section", "feat")), P(("section", "feat"), "dp")),
        check_vma=False,
    )
```

```python
import functools

import jax
import jax.numpy as jnp
from jax import lax
from jax.experimental import pallas as pl
from jax.experimental.pallas import tpu as pltpu
from jax.sharding import PartitionSpec as P

MESH = pl.DeviceIdType.MESH
BF16 = jnp.bfloat16
F32 = jnp.float32

BLOCK = 128
TILE = 128
SLOTS = 2
HALVES = 2
PART = 8
Z, Y = 8, 4
GROUP_ORDER = (6, 5, 7, 2, 4, 1, 3, 0)
GROUP_NEAR = (1, 3, 4, 2, 5, 7, 6)
Z_ORDER = (4, 3, 5, 2, 6, 1, 7, 0)
Z_NEAR = (1, 7, 2, 6, 3, 5, 4)
EARLY = 4
CHUNK = 2
CHORE_TIME, STEP_TIME = 0.5, 0.7

norm_eps = 1e-06


def dot_nn(a, b):
    return lax.dot_general(a, b, (((1,), (0,)), ((), ())), preferred_element_type=F32)


def dot_nt(a, b):
    return lax.dot_general(a, b, (((1,), (1,)), ((), ())), preferred_element_type=F32)


def block_at(ids_ref, slot, tile, blocks):
    return lax.rem(lax.max(ids_ref[slot, tile], 0), blocks)


class Place:
    def __init__(self):
        dp, feat = lax.axis_index("dp"), lax.axis_index("feat")
        self.xl = lax.axis_index("section")
        self.z, self.xh = dp // 2, dp % 2
        self.y, self.core = feat // 2, feat % 2

    def device(self, xl=None, z=None, xh=None, y=None, core=None):
        xl = self.xl if xl is None else xl
        z = self.z if z is None else z
        xh = self.xh if xh is None else xh
        y = self.y if y is None else y
        core = self.core if core is None else core
        return (xl, z * 2 + xh, y * 2 + core)

    def sibling(self):
        return self.device(core=1 - self.core)

    def x_partner(self):
        return self.device(xh=1 - self.xh)

    def group_chip(self, code, sign):
        xl = (self.xl + code // Y) % 2
        y = (self.y + sign * (code % Y) + Y) % Y
        return xl, y

    def group_device(self, code):
        xl, y = self.group_chip(code, 1)
        return self.device(xl=xl, y=y)

    def z_device(self, step):
        return self.device(z=(self.z + step) % Z)

    def dp_device(self, code):
        return self.device(z=(self.z + code // 2) % Z, xh=(self.xh + code % 2) % 2)


def exchange_kernel(
    ids_ref,
    rows_hbm,
    b_enc_hbm,
    ctx_hbm,
    w_out_hbm,
    resid_hbm,
    w_enc_hbm,
    w_dec_hbm,
    stream_out,
    gp_out,
    codes_out,
    go_out,
    ctx_ref,
    w_out_ref,
    rows_ref,
    b_enc_ref,
    w_enc,
    w_dec,
    resid,
    enc_t,
    dec_t,
    cols,
    a_part,
    a_core,
    a_sum,
    a_in,
    d_part,
    d_core,
    d_sum,
    d_in,
    c_part,
    c_x,
    c_sum,
    c_in,
    e_part,
    e_x,
    e_sum,
    e_in,
    stream,
    go,
    codes,
    gp,
    power,
    power_core,
    power_in,
    local_sem,
    block_sem,
    out_sem,
    s_sem,
    r_sem,
):
    at = Place()
    me = at
    full_width = w_out_ref.shape[0] * lax.axis_size("dp")
    half_rows = w_out_ref.shape[0] // 2

    barrier = pltpu.get_barrier_semaphore()
    friends = [at.sibling()]
    friends += [at.group_device(code) for code in range(1, 8)]
    friends += [at.dp_device(code) for code in range(1, 16)]
    for friend in friends:
        pl.semaphore_signal(barrier, inc=1, device_id=friend, device_id_type=MESH)

    def block_load(src, dst, number, block):
        lanes = pl.ds(pl.multiple_of(block * BLOCK, BLOCK), BLOCK)
        return pltpu.make_async_copy(
            src.at[:, lanes], dst.at[block], block_sem.at[number, block]
        )

    def start_blocks(src, dst, number):
        def one(block, carry):
            block_load(src, dst, number, block).start()
            return carry

        lax.fori_loop(0, dst.shape[0], one, 0)

    def wait_blocks(src, dst, number):
        def one(block, carry):
            block_load(src, dst, number, block).wait()
            return carry

        lax.fori_loop(0, dst.shape[0], one, 0)

    loads = [
        pltpu.make_async_copy(src, dst, local_sem.at[number])
        for number, (src, dst) in enumerate(
            (
                (ctx_hbm, ctx_ref),
                (w_out_hbm, w_out_ref),
                (resid_hbm, resid),
                (rows_hbm, rows_ref),
                (b_enc_hbm, b_enc_ref),
            )
        )
    ]
    for load in loads:
        load.start()
    start_blocks(w_enc_hbm, w_enc, 0)
    start_blocks(w_dec_hbm, w_dec, 1)

    count = [0]
    sent = []

    def send(src, dst, device):
        slot = count[0]
        count[0] += 1
        copy = pltpu.make_async_remote_copy(
            src_ref=src,
            dst_ref=dst,
            send_sem=s_sem.at[slot],
            recv_sem=r_sem.at[slot],
            device_id=device,
            device_id_type=MESH,
        )
        copy.start()
        sent.append(copy)
        return copy

    def columns_of(ref, tile, slot):
        return ref[block_at(ids_ref, slot, tile, ref.shape[0])]

    def rows_of(value):
        return value.reshape(2, half_rows, TILE)


    def group_part(h, spot, product, part):
        xl, y = at.group_chip(GROUP_ORDER[spot], 1)
        value = rows_of(product(xl * Y + y).astype(BF16))
        part[h, 0, spot] = value[0]
        part[h, 1, spot] = value[1]

    def group_reduce(h, product, part, core_in, total, arrived):
        copies = []
        for first in range(0, PART, 2):
            spots = pl.ds(first, 2)
            if product is not None:
                group_part(h, first, product, part)
                group_part(h, first + 1, product, part)
            copies.append(
                send(part.at[h, 1 - me.core, spots], core_in.at[h, spots], at.sibling())
            )
        yield 1.5
        copies_on = []
        for spot, code in enumerate(GROUP_ORDER):
            if spot % 2 == 0:
                copies[spot // 2].wait_recv()
            value = part[h, me.core, spot].astype(F32) + core_in[h, spot].astype(F32)
            if code == 0:
                own = value
                continue
            total[h, spot] = value.astype(BF16)
            copies_on.append(
                send(total.at[h, spot], arrived.at[h, code - 1], at.group_device(code))
            )
        yield 5.0
        for copy, code in zip(copies_on, GROUP_ORDER):
            copy.wait_recv()
            own += arrived[h, code - 1].astype(F32)
        return own

    def group_gather(h, value, table):
        mine = me.xl * Y + me.y
        table[h, mine, me.core] = value
        region = table.at[h, mine, me.core]
        copies = [send(region, region, at.group_device(code)) for code in GROUP_NEAR]
        forwards = [send(region, region, at.sibling())]
        yield 5.0
        for copy, code in zip(copies, GROUP_NEAR):
            copy.wait_recv()
            xl, y = at.group_chip(code, -1)
            region = table.at[h, xl * Y + y, me.core]
            forwards.append(send(region, region, at.sibling()))
        yield 1.5
        for copy in forwards:
            copy.wait_recv()

    def dp_reduce(h, product, part, x_in, total, arrived):
        copies = []
        for first in range(0, PART, 2):
            for spot in (first, first + 1):
                pair = product((me.z + Z_ORDER[spot]) % Z).astype(BF16)
                part[h, 0, spot] = pair[:BLOCK]
                part[h, 1, spot] = pair[BLOCK:]
            spots = pl.ds(first, 2)
            copies.append(
                send(part.at[h, 1 - me.xh, spots], x_in.at[h, spots], at.x_partner())
            )
        yield 4.0
        copies_on = []
        for spot, step in enumerate(Z_ORDER):
            if spot % 2 == 0:
                copies[spot // 2].wait_recv()
            value = part[h, me.xh, spot].astype(F32) + x_in[h, spot].astype(F32)
            if step == 0:
                own = value
                continue
            total[h, spot] = value.astype(BF16)
            copies_on.append(
                send(total.at[h, spot], arrived.at[h, step - 1], at.z_device(step))
            )
        yield 6.0
        for copy, step in zip(copies_on, Z_ORDER):
            copy.wait_recv()
            own += arrived[h, step - 1].astype(F32)
        return own

    def dp_gather(h, value, table):
        table[h, me.z, me.xh] = value
        region = table.at[h, me.z, me.xh]
        copies = [send(region, region, at.z_device(step)) for step in Z_NEAR]
        forwards = [send(region, region, at.x_partner())]
        yield 6.0
        for copy, step in zip(copies, Z_NEAR):
            copy.wait_recv()
            region = table.at[h, (me.z - step + Z) % Z, me.xh]
            forwards.append(send(region, region, at.x_partner()))
        yield 3.0
        for copy in forwards:
            copy.wait_recv()

    outs = []

    def write_out(h, table, out, number):
        copy = pltpu.make_async_copy(
            table.at[h], out.at[h], out_sem.at[h * 4 + number]
        )
        copy.start()
        outs.append(copy)

    def half(h):
        attn = yield from group_reduce(h, None, a_part, a_core, a_sum, a_in)
        power[h] = jnp.sum(attn * attn, axis=0, keepdims=True)
        copy = send(power.at[h], power_core.at[h], at.sibling())
        yield 1.5
        copy.wait_recv()
        power_in[h, 0] = power[h] + power_core[h]
        copies = [
            send(power_in.at[h, 0], power_in.at[h, code], at.dp_device(code))
            for code in range(1, 16)
        ]
        yield 4.5
        for copy in copies:
            copy.wait_recv()
        row_power = power_in[h, 0]
        for code in range(1, 16):
            row_power += power_in[h, code]
        inv_rms = lax.rsqrt(row_power / full_width + norm_eps)
        rows = pl.ds(pl.multiple_of(me.core * half_rows, 16), half_rows)
        tile = h * PART + me.xl * Y + me.y
        lanes = pl.ds(pl.multiple_of(tile * TILE, TILE), TILE)
        value = resid[rows, lanes].astype(F32) + attn * inv_rms * cols[0, rows, :]
        mine = value.astype(BF16)
        yield from group_gather(h, mine, stream)
        write_out(h, stream, stream_out, 0)

        ensure(0, h)

        def encode(tile):
            rows = stream[h, tile].reshape(2 * half_rows, TILE)
            return dot_nn(enc_t[h * PART + tile], rows)

        pre = yield from dp_reduce(h, encode, c_part, c_x, c_sum, c_in)
        own_tile = h * PART + me.z
        alive = lax.min(lax.max(ids_ref[me.xh, own_tile] + 1, 0), 1).astype(F32)
        bias = b_enc_ref[block_at(ids_ref, me.xh, own_tile, b_enc_ref.shape[0])]
        bias = jnp.broadcast_to(bias, (BLOCK, TILE))
        pre = pre + bias.T
        sigmoid = 1.0 / (1.0 + jnp.exp(-pre))
        code_values = (pre * sigmoid * alive).astype(BF16)
        slope = sigmoid * (1.0 + pre * (1.0 - sigmoid)) * alive
        yield from dp_gather(h, code_values, codes)
        write_out(h, codes, codes_out, 1)

        if 1 not in waited:
            waited.add(1)
            wait_blocks(w_dec_hbm, w_dec, 1)

        def decode(tile):
            pair = codes[h, tile]
            return dot_nn(columns_of(w_dec, h * PART + tile, 0), pair[0]) + dot_nn(
                columns_of(w_dec, h * PART + tile, 1), pair[1]
            )

        rebuilt = yield from group_reduce(h, decode, d_part, d_core, d_sum, d_in)
        grad_out = (rebuilt + cols[1, rows, :] - mine.astype(F32)) / TILE
        yield from group_gather(h, grad_out.astype(BF16), go)
        write_out(h, go, go_out, 2)

        ensure(1, h)

        def backward(tile):
            rows = go[h, tile].reshape(2 * half_rows, TILE)
            return dot_nn(dec_t[h * PART + tile], rows)

        back = yield from dp_reduce(h, backward, e_part, e_x, e_sum, e_in)
        yield from dp_gather(h, (back * slope).astype(BF16), gp)
        write_out(h, gp, gp_out, 3)

    def turn(table, out, first):
        def one(tile, carry):
            out[tile, 0:BLOCK, :] = columns_of(table, tile, 0).T
            out[tile, BLOCK : 2 * BLOCK, :] = columns_of(table, tile, 1).T
            return carry

        lax.fori_loop(first, first + CHUNK, one, 0)

    waited = set()
    chores = [
        (number, first)
        for number in range(2)
        for first in range(0, HALVES * PART, CHUNK)
    ]

    def chore():
        number, first = chores.pop(0)
        src, table, out = (
            (w_enc_hbm, w_enc, enc_t),
            (w_dec_hbm, w_dec, dec_t),
        )[number]
        if number not in waited:
            waited.add(number)
            wait_blocks(src, table, number)
        turn(table, out, first)

    def ensure(number, h):
        while chores and chores[0] < (number, (h + 1) * PART):
            chore()

    for load in loads:
        load.wait()
    for h in range(HALVES):

        def attention(tile, h=h):
            rows = ctx_ref[pl.ds(pl.multiple_of((h * PART + tile) * TILE, TILE), TILE), :]
            return dot_nt(w_out_ref[...], rows)

        for spot in range(PART):
            group_part(h, spot, attention, a_part)
    for number in range(2):
        row = rows_ref[pl.ds(number, 1), :]
        cols[number] = jnp.broadcast_to(row, (TILE, row.shape[1])).T
    for _ in range(EARLY):
        chore()
    pl.semaphore_wait(barrier, len(friends))
    runs = [half(h) for h in range(HALVES)]
    due = [float(h) for h in range(HALVES)]
    clock = 0.0
    started = False
    while runs:
        h = min(range(len(runs)), key=lambda i: due[i])
        while chores and clock + CHORE_TIME < due[h] and started:
            chore()
            clock += CHORE_TIME
        clock = max(clock, due[h]) + STEP_TIME
        try:
            due[h] = clock + next(runs[h])
        except StopIteration:
            del runs[h], due[h]
        started = True
    for copy in sent:
        copy.wait_send()
    for copy in outs:
        copy.wait()


SENDS = HALVES * (4 * (4 + 7 + 15) + 16)


def exchange(ids, ctx, w_out_t, gain_bias, b_enc, resid_t, w_enc, w_dec_t):
    width = w_out_t.shape[0]
    half_rows = width // 2
    blocks_here = w_enc.shape[1] // BLOCK
    tiles = HALVES * PART
    hbm = pl.BlockSpec(memory_space=pl.ANY)
    wide = (HALVES, PART, 2, half_rows, TILE)
    narrow = (HALVES, PART, SLOTS, BLOCK, TILE)
    group_sets = [
        pltpu.VMEM((HALVES, 2, PART, half_rows, TILE), BF16),
        pltpu.VMEM((HALVES, PART, half_rows, TILE), BF16),
        pltpu.VMEM((HALVES, PART, half_rows, TILE), BF16),
        pltpu.VMEM((HALVES, 7, half_rows, TILE), BF16),
    ]
    dp_sets = [
        pltpu.VMEM((HALVES, SLOTS, PART, BLOCK, TILE), BF16),
        pltpu.VMEM((HALVES, PART, BLOCK, TILE), BF16),
        pltpu.VMEM((HALVES, PART, BLOCK, TILE), BF16),
        pltpu.VMEM((HALVES, 7, BLOCK, TILE), BF16),
    ]
    scratch = [
        pltpu.VMEM(ctx.shape, BF16),
        pltpu.VMEM(w_out_t.shape, BF16),
        pltpu.VMEM(gain_bias.shape, F32),
        pltpu.VMEM(b_enc.shape, F32),
        pltpu.VMEM((blocks_here, width, BLOCK), BF16),
        pltpu.VMEM((blocks_here, width, BLOCK), BF16),
        pltpu.VMEM(resid_t.shape, BF16),
        pltpu.VMEM((tiles, SLOTS * BLOCK, width), BF16),
        pltpu.VMEM((tiles, SLOTS * BLOCK, width), BF16),
        pltpu.VMEM((2, width, TILE), F32),
        *group_sets,
        *group_sets,
        *dp_sets,
        *dp_sets,
        pltpu.VMEM(wide, BF16),
        pltpu.VMEM(wide, BF16),
        pltpu.VMEM(narrow, BF16),
        pltpu.VMEM(narrow, BF16),
        pltpu.VMEM((HALVES, 1, TILE), F32),
        pltpu.VMEM((HALVES, 1, TILE), F32),
        pltpu.VMEM((HALVES, 16, 1, TILE), F32),
        pltpu.SemaphoreType.DMA((5,)),
        pltpu.SemaphoreType.DMA((2, blocks_here)),
        pltpu.SemaphoreType.DMA((HALVES * 4,)),
        pltpu.SemaphoreType.DMA((SENDS,)),
        pltpu.SemaphoreType.DMA((SENDS,)),
    ]
    return pl.pallas_call(
        exchange_kernel,
        out_shape=(
            jax.ShapeDtypeStruct(wide, BF16),
            jax.ShapeDtypeStruct(narrow, BF16),
            jax.ShapeDtypeStruct(narrow, BF16),
            jax.ShapeDtypeStruct(wide, BF16),
        ),
        in_specs=[pl.BlockSpec(memory_space=pltpu.SMEM)] + [hbm] * 7,
        out_specs=(hbm,) * 4,
        scratch_shapes=scratch,
        compiler_params=pltpu.CompilerParams(
            collective_id=0, has_side_effects=True, vmem_limit_bytes=52 << 20
        ),
    )(ids, gain_bias, b_enc, ctx, w_out_t, resid_t, w_enc, w_dec_t)


def gradient_kernel(
    ids_ref,
    stream_hbm,
    gp_hbm,
    codes_hbm,
    go_hbm,
    enc_out,
    dec_out,
    stream,
    gp,
    codes,
    go,
    total,
    result,
    in_sem,
    out_sem,
):
    loads = [
        pltpu.make_async_copy(src, dst, in_sem.at[number])
        for number, (src, dst) in enumerate(
            ((codes_hbm, codes), (go_hbm, go), (stream_hbm, stream), (gp_hbm, gp))
        )
    ]
    for load in loads:
        load.start()
    total[...] = jnp.zeros_like(total)
    width, features = total.shape[1:]
    share = features // 4
    writes = []
    for number, (left, right, out) in enumerate(
        ((go, codes, dec_out), (stream, gp, enc_out))
    ):
        loads[2 * number].wait()
        loads[2 * number + 1].wait()

        def one(tile, carry, number=number, left=left, right=right):
            h, j = tile // PART, tile % PART
            terms = dot_nt(
                left[h, j].reshape(width, TILE), right[h, j].reshape(SLOTS * BLOCK, TILE)
            )
            for slot in range(SLOTS):
                block = block_at(ids_ref, slot, tile, features // BLOCK)
                lanes = pl.ds(pl.multiple_of(block * BLOCK, BLOCK), BLOCK)
                total[number, :, lanes] += terms[:, slot * BLOCK : (slot + 1) * BLOCK]
            return carry

        lax.fori_loop(0, HALVES * PART, one, 0, unroll=4)
        for quarter in range(4):
            lanes = pl.ds(quarter * share, share)
            result[number, :, lanes] = total[number, :, lanes].astype(BF16)
            write = pltpu.make_async_copy(
                result.at[number, :, lanes], out.at[:, lanes], out_sem.at[number, quarter]
            )
            write.start()
            writes.append(write)
    for write in writes:
        write.wait()


def gradients(ids, stream, gp, codes, go, shape):
    hbm = pl.BlockSpec(memory_space=pl.ANY)
    return pl.pallas_call(
        gradient_kernel,
        out_shape=(jax.ShapeDtypeStruct(shape, BF16),) * 2,
        in_specs=[pl.BlockSpec(memory_space=pltpu.SMEM)] + [hbm] * 4,
        out_specs=(hbm,) * 2,
        scratch_shapes=[
            pltpu.VMEM(stream.shape, BF16),
            pltpu.VMEM(gp.shape, BF16),
            pltpu.VMEM(codes.shape, BF16),
            pltpu.VMEM(go.shape, BF16),
            pltpu.VMEM((2, *shape), F32),
            pltpu.VMEM((2, *shape), BF16),
            pltpu.SemaphoreType.DMA((4,)),
            pltpu.SemaphoreType.DMA((2, 4)),
        ],
        compiler_params=pltpu.CompilerParams(vmem_limit_bytes=52 << 20),
    )(ids, stream, gp, codes, go)


def body(context, w_out, residual, norm_gain, w_enc, b_enc, w_dec, b_dec, block_slots):
    ids = block_slots[:, 0, :].T
    stream, gp, codes, go = exchange(
        ids,
        context,
        w_out.T,
        jnp.stack([norm_gain, b_dec]),
        b_enc.reshape(-1, 1, BLOCK),
        residual.T,
        w_enc,
        w_dec.T,
    )
    grad_enc, grad_dec_t = gradients(ids, stream, gp, codes, go, w_enc.shape)
    return grad_enc, grad_dec_t.T


def solution(mesh):
    placed = (
        P(None, ("section", "feat")),
        P(("section", "feat"), "dp"),
        P(None, "dp"),
        P("dp"),
        P("dp", ("section", "feat")),
        P(("section", "feat")),
        P(("section", "feat"), "dp"),
        P("dp"),
        P(None, ("section", "feat"), None),
    )
    return jax.shard_map(
        body,
        mesh=mesh,
        in_specs=placed,
        out_specs=(P("dp", ("section", "feat")), P(("section", "feat"), "dp")),
        check_vma=False,
    )
```

```python
import functools

import jax
import jax.numpy as jnp
from jax import lax
from jax.experimental import pallas as pl
from jax.experimental.pallas import tpu as pltpu
from jax.sharding import PartitionSpec as P

MESH = pl.DeviceIdType.MESH
BF16 = jnp.bfloat16
F32 = jnp.float32

BLOCK = 128
TILE = 128
SLOTS = 2
HALVES = 2
PART = 8
Z, Y = 8, 4
GROUP_ORDER = (6, 5, 7, 2, 4, 1, 3, 0)
GROUP_NEAR = (1, 3, 4, 2, 5, 7, 6)
Z_ORDER = (4, 3, 5, 2, 6, 1, 7, 0)
Z_NEAR = (1, 7, 2, 6, 3, 5, 4)
EARLY = 4
CHUNK = 2
CHORE_TIME, STEP_TIME = 0.5, 0.7

norm_eps = 1e-06


def dot_nn(a, b):
    return lax.dot_general(a, b, (((1,), (0,)), ((), ())), preferred_element_type=F32)


def dot_nt(a, b):
    return lax.dot_general(a, b, (((1,), (1,)), ((), ())), preferred_element_type=F32)


def block_at(ids_ref, slot, tile, blocks):
    return lax.rem(lax.max(ids_ref[slot, tile], 0), blocks)


class Place:
    def __init__(self):
        dp, feat = lax.axis_index("dp"), lax.axis_index("feat")
        self.xl = lax.axis_index("section")
        self.z, self.xh = dp // 2, dp % 2
        self.y, self.core = feat // 2, feat % 2

    def device(self, xl=None, z=None, xh=None, y=None, core=None):
        xl = self.xl if xl is None else xl
        z = self.z if z is None else z
        xh = self.xh if xh is None else xh
        y = self.y if y is None else y
        core = self.core if core is None else core
        return (xl, z * 2 + xh, y * 2 + core)

    def sibling(self):
        return self.device(core=1 - self.core)

    def x_partner(self):
        return self.device(xh=1 - self.xh)

    def group_chip(self, code, sign):
        xl = (self.xl + code // Y) % 2
        y = (self.y + sign * (code % Y) + Y) % Y
        return xl, y

    def group_device(self, code):
        xl, y = self.group_chip(code, 1)
        return self.device(xl=xl, y=y)

    def z_device(self, step):
        return self.device(z=(self.z + step) % Z)

    def dp_device(self, code):
        return self.device(z=(self.z + code // 2) % Z, xh=(self.xh + code % 2) % 2)


def exchange_kernel(
    ids_ref,
    gain_hbm,
    b_dec_hbm,
    b_enc_hbm,
    ctx_hbm,
    w_out_hbm,
    resid_hbm,
    w_enc_hbm,
    w_dec_hbm,
    stream_out,
    gp_out,
    codes_out,
    go_out,
    ctx_ref,
    w_out_ref,
    gain_ref,
    b_dec_ref,
    b_enc_ref,
    w_enc,
    w_dec,
    resid,
    enc_t,
    dec_t,
    cols,
    a_part,
    a_core,
    a_sum,
    a_in,
    d_part,
    d_core,
    d_sum,
    d_in,
    c_part,
    c_x,
    c_sum,
    c_in,
    e_part,
    e_x,
    e_sum,
    e_in,
    stream,
    go,
    codes,
    gp,
    power,
    power_core,
    power_in,
    local_sem,
    block_sem,
    out_sem,
    s_sem,
    r_sem,
):
    at = Place()
    me = at
    full_width = w_out_ref.shape[0] * lax.axis_size("dp")
    half_rows = w_out_ref.shape[0] // 2

    barrier = pltpu.get_barrier_semaphore()
    friends = [at.sibling()]
    friends += [at.group_device(code) for code in range(1, 8)]
    friends += [at.dp_device(code) for code in range(1, 16)]
    for friend in friends:
        pl.semaphore_signal(barrier, inc=1, device_id=friend, device_id_type=MESH)

    def block_load(src, dst, number, block):
        lanes = pl.ds(pl.multiple_of(block * BLOCK, BLOCK), BLOCK)
        return pltpu.make_async_copy(
            src.at[:, lanes], dst.at[block], block_sem.at[number, block]
        )

    def start_blocks(src, dst, number):
        def one(block, carry):
            block_load(src, dst, number, block).start()
            return carry

        lax.fori_loop(0, dst.shape[0], one, 0)

    def wait_blocks(src, dst, number):
        def one(block, carry):
            block_load(src, dst, number, block).wait()
            return carry

        lax.fori_loop(0, dst.shape[0], one, 0)

    loads = [
        pltpu.make_async_copy(src, dst, local_sem.at[number])
        for number, (src, dst) in enumerate(
            (
                (ctx_hbm, ctx_ref),
                (w_out_hbm, w_out_ref),
                (resid_hbm, resid),
                (gain_hbm, gain_ref),
                (b_dec_hbm, b_dec_ref),
                (b_enc_hbm, b_enc_ref),
            )
        )
    ]
    for load in loads:
        load.start()
    start_blocks(w_enc_hbm, w_enc, 0)
    start_blocks(w_dec_hbm, w_dec, 1)

    count = [0]
    sent = []

    def send(src, dst, device):
        slot = count[0]
        count[0] += 1
        copy = pltpu.make_async_remote_copy(
            src_ref=src,
            dst_ref=dst,
            send_sem=s_sem.at[slot],
            recv_sem=r_sem.at[slot],
            device_id=device,
            device_id_type=MESH,
        )
        copy.start()
        sent.append(copy)
        return copy

    def columns_of(ref, tile, slot):
        return ref[block_at(ids_ref, slot, tile, ref.shape[0])]

    def rows_of(value):
        return value.reshape(2, half_rows, TILE)


    def group_part(h, spot, product, part):
        xl, y = at.group_chip(GROUP_ORDER[spot], 1)
        value = rows_of(product(xl * Y + y).astype(BF16))
        part[h, 0, spot] = value[0]
        part[h, 1, spot] = value[1]

    def group_reduce(h, product, part, core_in, total, arrived):
        copies = []
        for first in range(0, PART, 2):
            spots = pl.ds(first, 2)
            if product is not None:
                group_part(h, first, product, part)
                group_part(h, first + 1, product, part)
            copies.append(
                send(part.at[h, 1 - me.core, spots], core_in.at[h, spots], at.sibling())
            )
        yield 1.5
        copies_on = []
        for spot, code in enumerate(GROUP_ORDER):
            if spot % 2 == 0:
                copies[spot // 2].wait_recv()
            value = part[h, me.core, spot].astype(F32) + core_in[h, spot].astype(F32)
            if code == 0:
                own = value
                continue
            total[h, spot] = value.astype(BF16)
            copies_on.append(
                send(total.at[h, spot], arrived.at[h, code - 1], at.group_device(code))
            )
        yield 5.0
        for copy, code in zip(copies_on, GROUP_ORDER):
            copy.wait_recv()
            own += arrived[h, code - 1].astype(F32)
        return own

    def group_gather(h, value, table):
        mine = me.xl * Y + me.y
        table[h, mine, me.core] = value
        region = table.at[h, mine, me.core]
        copies = [send(region, region, at.group_device(code)) for code in GROUP_NEAR]
        forwards = [send(region, region, at.sibling())]
        yield 5.0
        for copy, code in zip(copies, GROUP_NEAR):
            copy.wait_recv()
            xl, y = at.group_chip(code, -1)
            region = table.at[h, xl * Y + y, me.core]
            forwards.append(send(region, region, at.sibling()))
        yield 1.5
        for copy in forwards:
            copy.wait_recv()

    def dp_reduce(h, product, part, x_in, total, arrived):
        copies = []
        for first in range(0, PART, 2):
            for spot in (first, first + 1):
                pair = product((me.z + Z_ORDER[spot]) % Z).astype(BF16)
                part[h, 0, spot] = pair[:BLOCK]
                part[h, 1, spot] = pair[BLOCK:]
            spots = pl.ds(first, 2)
            copies.append(
                send(part.at[h, 1 - me.xh, spots], x_in.at[h, spots], at.x_partner())
            )
        yield 4.0
        copies_on = []
        for spot, step in enumerate(Z_ORDER):
            if spot % 2 == 0:
                copies[spot // 2].wait_recv()
            value = part[h, me.xh, spot].astype(F32) + x_in[h, spot].astype(F32)
            if step == 0:
                own = value
                continue
            total[h, spot] = value.astype(BF16)
            copies_on.append(
                send(total.at[h, spot], arrived.at[h, step - 1], at.z_device(step))
            )
        yield 6.0
        for copy, step in zip(copies_on, Z_ORDER):
            copy.wait_recv()
            own += arrived[h, step - 1].astype(F32)
        return own

    def dp_gather(h, value, table):
        table[h, me.z, me.xh] = value
        region = table.at[h, me.z, me.xh]
        copies = [send(region, region, at.z_device(step)) for step in Z_NEAR]
        forwards = [send(region, region, at.x_partner())]
        yield 6.0
        for copy, step in zip(copies, Z_NEAR):
            copy.wait_recv()
            region = table.at[h, (me.z - step + Z) % Z, me.xh]
            forwards.append(send(region, region, at.x_partner()))
        yield 3.0
        for copy in forwards:
            copy.wait_recv()

    outs = []

    def write_out(h, table, out, number):
        copy = pltpu.make_async_copy(
            table.at[h], out.at[h], out_sem.at[h * 4 + number]
        )
        copy.start()
        outs.append(copy)

    def half(h):
        attn = yield from group_reduce(h, None, a_part, a_core, a_sum, a_in)
        power[h] = jnp.sum(attn * attn, axis=0, keepdims=True)
        copy = send(power.at[h], power_core.at[h], at.sibling())
        yield 1.5
        copy.wait_recv()
        power_in[h, 0] = power[h] + power_core[h]
        copies = [
            send(power_in.at[h, 0], power_in.at[h, code], at.dp_device(code))
            for code in range(1, 16)
        ]
        yield 4.5
        for copy in copies:
            copy.wait_recv()
        row_power = power_in[h, 0]
        for code in range(1, 16):
            row_power += power_in[h, code]
        inv_rms = lax.rsqrt(row_power / full_width + norm_eps)
        rows = pl.ds(pl.multiple_of(me.core * half_rows, 16), half_rows)
        tile = h * PART + me.xl * Y + me.y
        lanes = pl.ds(pl.multiple_of(tile * TILE, TILE), TILE)
        value = resid[rows, lanes].astype(F32) + attn * inv_rms * cols[0, rows, :]
        mine = value.astype(BF16)
        yield from group_gather(h, mine, stream)
        write_out(h, stream, stream_out, 0)

        ensure(0, h)

        def encode(tile):
            rows = stream[h, tile].reshape(2 * half_rows, TILE)
            return dot_nn(enc_t[h * PART + tile], rows)

        pre = yield from dp_reduce(h, encode, c_part, c_x, c_sum, c_in)
        own_tile = h * PART + me.z
        alive = lax.min(lax.max(ids_ref[me.xh, own_tile] + 1, 0), 1).astype(F32)
        bias = b_enc_ref[block_at(ids_ref, me.xh, own_tile, b_enc_ref.shape[0])]
        bias = jnp.broadcast_to(bias, (BLOCK, TILE))
        pre = pre + bias.T
        sigmoid = 1.0 / (1.0 + jnp.exp(-pre))
        code_values = (pre * sigmoid * alive).astype(BF16)
        slope = sigmoid * (1.0 + pre * (1.0 - sigmoid)) * alive
        yield from dp_gather(h, code_values, codes)
        write_out(h, codes, codes_out, 1)

        if 1 not in waited:
            waited.add(1)
            wait_blocks(w_dec_hbm, w_dec, 1)

        def decode(tile):
            pair = codes[h, tile]
            return dot_nn(columns_of(w_dec, h * PART + tile, 0), pair[0]) + dot_nn(
                columns_of(w_dec, h * PART + tile, 1), pair[1]
            )

        rebuilt = yield from group_reduce(h, decode, d_part, d_core, d_sum, d_in)
        grad_out = (rebuilt + cols[1, rows, :] - mine.astype(F32)) / TILE
        yield from group_gather(h, grad_out.astype(BF16), go)
        write_out(h, go, go_out, 2)

        ensure(1, h)

        def backward(tile):
            rows = go[h, tile].reshape(2 * half_rows, TILE)
            return dot_nn(dec_t[h * PART + tile], rows)

        back = yield from dp_reduce(h, backward, e_part, e_x, e_sum, e_in)
        yield from dp_gather(h, (back * slope).astype(BF16), gp)
        write_out(h, gp, gp_out, 3)

    def turn(table, out, first):
        def one(tile, carry):
            out[tile, 0:BLOCK, :] = columns_of(table, tile, 0).T
            out[tile, BLOCK : 2 * BLOCK, :] = columns_of(table, tile, 1).T
            return carry

        lax.fori_loop(first, first + CHUNK, one, 0)

    waited = set()
    chores = [
        (number, first)
        for number in range(2)
        for first in range(0, HALVES * PART, CHUNK)
    ]

    def chore():
        number, first = chores.pop(0)
        src, table, out = (
            (w_enc_hbm, w_enc, enc_t),
            (w_dec_hbm, w_dec, dec_t),
        )[number]
        if number not in waited:
            waited.add(number)
            wait_blocks(src, table, number)
        turn(table, out, first)

    def ensure(number, h):
        while chores and chores[0] < (number, (h + 1) * PART):
            chore()

    for load in loads:
        load.wait()
    for h in range(HALVES):

        def attention(tile, h=h):
            rows = ctx_ref[pl.ds(pl.multiple_of((h * PART + tile) * TILE, TILE), TILE), :]
            return dot_nt(w_out_ref[...], rows)

        for spot in range(PART):
            group_part(h, spot, attention, a_part)
    for number, ref in enumerate((gain_ref, b_dec_ref)):
        row = ref[...].reshape(1, -1)
        cols[number] = jnp.broadcast_to(row, (TILE, row.shape[1])).T
    for _ in range(EARLY):
        chore()
    pl.semaphore_wait(barrier, len(friends))
    runs = [half(h) for h in range(HALVES)]
    due = [float(h) for h in range(HALVES)]
    clock = 0.0
    started = False
    while runs:
        h = min(range(len(runs)), key=lambda i: due[i])
        while chores and clock + CHORE_TIME < due[h] and started:
            chore()
            clock += CHORE_TIME
        clock = max(clock, due[h]) + STEP_TIME
        try:
            due[h] = clock + next(runs[h])
        except StopIteration:
            del runs[h], due[h]
        started = True
    for copy in sent:
        copy.wait_send()
    for copy in outs:
        copy.wait()


SENDS = HALVES * (4 * (4 + 7 + 15) + 16)


def exchange(ids, ctx, w_out_t, gain, b_dec, b_enc, resid_t, w_enc, w_dec_t):
    width = w_out_t.shape[0]
    half_rows = width // 2
    blocks_here = w_enc.shape[1] // BLOCK
    tiles = HALVES * PART
    hbm = pl.BlockSpec(memory_space=pltpu.HBM)
    wide = (HALVES, PART, 2, half_rows, TILE)
    narrow = (HALVES, PART, SLOTS, BLOCK, TILE)
    group_sets = [
        pltpu.VMEM((HALVES, 2, PART, half_rows, TILE), BF16),
        pltpu.VMEM((HALVES, PART, half_rows, TILE), BF16),
        pltpu.VMEM((HALVES, PART, half_rows, TILE), BF16),
        pltpu.VMEM((HALVES, 7, half_rows, TILE), BF16),
    ]
    dp_sets = [
        pltpu.VMEM((HALVES, SLOTS, PART, BLOCK, TILE), BF16),
        pltpu.VMEM((HALVES, PART, BLOCK, TILE), BF16),
        pltpu.VMEM((HALVES, PART, BLOCK, TILE), BF16),
        pltpu.VMEM((HALVES, 7, BLOCK, TILE), BF16),
    ]
    scratch = [
        pltpu.VMEM(ctx.shape, BF16),
        pltpu.VMEM(w_out_t.shape, BF16),
        pltpu.VMEM(gain.shape, F32),
        pltpu.VMEM(b_dec.shape, F32),
        pltpu.VMEM(b_enc.shape, F32),
        pltpu.VMEM((blocks_here, width, BLOCK), BF16),
        pltpu.VMEM((blocks_here, width, BLOCK), BF16),
        pltpu.VMEM(resid_t.shape, BF16),
        pltpu.VMEM((tiles, SLOTS * BLOCK, width), BF16),
        pltpu.VMEM((tiles, SLOTS * BLOCK, width), BF16),
        pltpu.VMEM((2, width, TILE), F32),
        *group_sets,
        *group_sets,
        *dp_sets,
        *dp_sets,
        pltpu.VMEM(wide, BF16),
        pltpu.VMEM(wide, BF16),
        pltpu.VMEM(narrow, BF16),
        pltpu.VMEM(narrow, BF16),
        pltpu.VMEM((HALVES, 1, TILE), F32),
        pltpu.VMEM((HALVES, 1, TILE), F32),
        pltpu.VMEM((HALVES, 16, 1, TILE), F32),
        pltpu.SemaphoreType.DMA((6,)),
        pltpu.SemaphoreType.DMA((2, blocks_here)),
        pltpu.SemaphoreType.DMA((HALVES * 4,)),
        pltpu.SemaphoreType.DMA((SENDS,)),
        pltpu.SemaphoreType.DMA((SENDS,)),
    ]
    return pl.pallas_call(
        exchange_kernel,
        out_shape=(
            jax.ShapeDtypeStruct(wide, BF16),
            jax.ShapeDtypeStruct(narrow, BF16),
            jax.ShapeDtypeStruct(narrow, BF16),
            jax.ShapeDtypeStruct(wide, BF16),
        ),
        in_specs=[pl.BlockSpec(memory_space=pltpu.SMEM)] + [hbm] * 8,
        out_specs=(hbm,) * 4,
        scratch_shapes=scratch,
        compiler_params=pltpu.CompilerParams(
            collective_id=0, has_side_effects=True, vmem_limit_bytes=60 << 20
        ),
    )(ids, gain, b_dec, b_enc, ctx, w_out_t, resid_t, w_enc, w_dec_t)


def gradient_kernel(
    ids_ref,
    stream_hbm,
    gp_hbm,
    codes_hbm,
    go_hbm,
    enc_out,
    dec_out,
    stream,
    gp,
    codes,
    go,
    total,
    result,
    in_sem,
    out_sem,
):
    loads = [
        pltpu.make_async_copy(src, dst, in_sem.at[number])
        for number, (src, dst) in enumerate(
            ((codes_hbm, codes), (go_hbm, go), (stream_hbm, stream), (gp_hbm, gp))
        )
    ]
    for load in loads:
        load.start()
    total[...] = jnp.zeros_like(total)
    width, features = total.shape[1:]
    share = features // 4
    writes = []
    for number, (left, right, out) in enumerate(
        ((go, codes, dec_out), (stream, gp, enc_out))
    ):
        loads[2 * number].wait()
        loads[2 * number + 1].wait()

        def one(tile, carry, number=number, left=left, right=right):
            h, j = tile // PART, tile % PART
            terms = dot_nt(
                left[h, j].reshape(width, TILE), right[h, j].reshape(SLOTS * BLOCK, TILE)
            )
            for slot in range(SLOTS):
                block = block_at(ids_ref, slot, tile, features // BLOCK)
                lanes = pl.ds(pl.multiple_of(block * BLOCK, BLOCK), BLOCK)
                total[number, :, lanes] += terms[:, slot * BLOCK : (slot + 1) * BLOCK]
            return carry

        lax.fori_loop(0, HALVES * PART, one, 0, unroll=4)
        for quarter in range(4):
            lanes = pl.ds(quarter * share, share)
            result[number, :, lanes] = total[number, :, lanes].astype(BF16)
            write = pltpu.make_async_copy(
                result.at[number, :, lanes], out.at[:, lanes], out_sem.at[number, quarter]
            )
            write.start()
            writes.append(write)
    for write in writes:
        write.wait()


def gradients(ids, stream, gp, codes, go, shape):
    hbm = pl.BlockSpec(memory_space=pltpu.HBM)
    return pl.pallas_call(
        gradient_kernel,
        out_shape=(jax.ShapeDtypeStruct(shape, BF16),) * 2,
        in_specs=[pl.BlockSpec(memory_space=pltpu.SMEM)] + [hbm] * 4,
        out_specs=(hbm,) * 2,
        scratch_shapes=[
            pltpu.VMEM(stream.shape, BF16),
            pltpu.VMEM(gp.shape, BF16),
            pltpu.VMEM(codes.shape, BF16),
            pltpu.VMEM(go.shape, BF16),
            pltpu.VMEM((2, *shape), F32),
            pltpu.VMEM((2, *shape), BF16),
            pltpu.SemaphoreType.DMA((4,)),
            pltpu.SemaphoreType.DMA((2, 4)),
        ],
        compiler_params=pltpu.CompilerParams(vmem_limit_bytes=60 << 20),
    )(ids, stream, gp, codes, go)


def body(context, w_out, residual, norm_gain, w_enc, b_enc, w_dec, b_dec, block_slots):
    ids = block_slots[:, 0, :].T
    stream, gp, codes, go = exchange(
        ids,
        context,
        w_out.T,
        norm_gain,
        b_dec,
        b_enc.reshape(-1, 1, BLOCK),
        residual.T,
        w_enc,
        w_dec.T,
    )
    grad_enc, grad_dec_t = gradients(ids, stream, gp, codes, go, w_enc.shape)
    return grad_enc, grad_dec_t.T


def solution(mesh):
    placed = (
        P(None, ("section", "feat")),
        P(("section", "feat"), "dp"),
        P(None, "dp"),
        P("dp"),
        P("dp", ("section", "feat")),
        P(("section", "feat")),
        P(("section", "feat"), "dp"),
        P("dp"),
        P(None, ("section", "feat"), None),
    )
    return jax.shard_map(
        body,
        mesh=mesh,
        in_specs=placed,
        out_specs=(P("dp", ("section", "feat")), P(("section", "feat"), "dp")),
        check_vma=False,
    )
```
